32 devices in a mesh: dp: 16 (over z, y, x), head: 2 (over core).
Axes of the slice: x: 2, y: 2, z: 4, core: 2. Of those that a mesh axis runs over, the one named last changes fastest.
Arguments:
- inputs: bfloat16 [64, 1024, 768], P('dp', None, 'head'), may hold values from -6 to 6
- lengths: int32 [64], P('dp'), may hold values from 64 to 1024, as said below
- gain_mix: bfloat16 [768], P('dp'), may hold values from 0.5 to 1.5
- w_value: bfloat16 [768, 768], P('dp', 'head'), may hold values from -0.21875 to 0.21875
- mix_table: bfloat16 [12, 1024, 1024], P('head', 'dp'), may hold values from -6 to 6
- w_out: bfloat16 [768, 768], P('head', 'dp'), may hold values from -1.5 to 1.5
- gain_feed: bfloat16 [768], P('dp'), may hold values from 0.5 to 1.5
- w_up: bfloat16 [768, 3072], P('dp', 'head'), may hold values from -0.21875 to 0.21875
- w_down: bfloat16 [3072, 768], P('head', 'dp'), may hold values from -0.109375 to 0.109375
- out_grad: bfloat16 [64, 1024, 768], P('dp', None, 'head'), may hold values from -6 to 6
Outputs:
- output: bfloat16 [64, 1024, 768], P('dp', None, 'head')
- input_grad: bfloat16 [64, 1024, 768], P('dp', None, 'head')
- gain_mix_grad: float32 [768], P('dp')
- value_grad: float32 [768, 768], P('dp', 'head')
- table_grad: float32 [12, 1024, 1024], P('head', 'dp')
- projection_grad: float32 [768, 768], P('head', 'dp')
- gain_feed_grad: float32 [768], P('dp')
- up_grad: float32 [768, 3072], P('dp', 'head')
- down_grad: float32 [3072, 768], P('head', 'dp')
The draws below stay inside these ranges and needn't reach their ends.
Inputs may be any that keep to these rules, and one draw needn't show every extreme that they name: `lengths`: each item's valid length; positions at or past it are padding. In every draw some item has exactly 1024 and some other exactly 64.
All inputs are finite; a program needn't handle non-finite values.
Results may differ from the reference program's by a relative error of at most 0.015.
Values may be sent and summed in bfloat16 or wider, within the bound.
No kernel may reach another device: no remote copies, remote signals or barrier semaphores. Data moves between devices by JAX's collectives and lax.ppermute only.
A program may use at most 448 MiB of HBM per device.

```python
from functools import partial
import jax
import jax.numpy as jnp
from jax import lax

D = 768
HEADS = 12
HEAD_DIM = 64
FF = 3072
SEQ = 1024
MINLEN = 64
SEQS = 64


def draw_lengths(key, part):
    key = jax.random.fold_in(key, 7)
    key_len, key_long, key_short = jax.random.split(key, 3)
    drawn = jax.random.randint(key_len, (SEQS,), MINLEN, SEQ + 1)
    longest = jax.random.randint(key_long, (), 0, SEQS)
    shortest = (longest + 1 + jax.random.randint(key_short, (), 0, SEQS - 1)) % SEQS
    slot_index = jnp.arange(SEQS)
    drawn = jnp.where(slot_index == longest, SEQ, drawn)
    drawn = jnp.where(slot_index == shortest, MINLEN, drawn)
    return drawn.astype(jnp.int32)


def levels(stream_key, shape, pieces, smallest, high):
    factor_of, own = 1.0, jax.random.fold_in(stream_key, 6)
    for position, shards_of in pieces:
        steps = jnp.exp(jax.random.uniform(jax.random.fold_in(own, position), (shards_of,), jnp.float32, smallest / len(pieces), high / len(pieces)))
        factor_of = factor_of * jnp.repeat(steps, shape[position] // shards_of).reshape([-1 if axis == position else 1 for axis in range(len(shape))])
    return factor_of


def noise(own_key, dims, spread, most, pieces=(), held_as=jnp.bfloat16):
    array = jax.random.normal(own_key, dims, jnp.float32) * spread
    if len(pieces) > 0:
        array = levels(own_key, dims, pieces, -0.22, 0.18) * array
    return jnp.clip(array, min=-most, max=most).astype(held_as)


def setup_inputs(seed: int = 0) -> dict:
    key_list = jax.random.split(jax.random.key(seed), 11)
    return {
        "inputs": noise(key_list[0], (SEQS, SEQ, D), 1.0, 6.0, ((0, 16), (2, 2))),
        "lengths": draw_lengths(jax.random.fold_in(key_list[10], 71), 0),
        "gain_mix": jnp.clip(1.0 + 0.1 * jax.random.normal(key_list[2], (D,), jnp.float32), 0.5, 1.5).astype(jnp.bfloat16),
        "w_value": noise(key_list[3], (D, D), D ** -0.5, 0.21875, ((0, 16), (1, 2))),
        "mix_table": noise(key_list[4], (HEADS, SEQ, SEQ), 1.5, 6.0, ((0, 2), (1, 16))),
        "w_out": noise(key_list[5], (D, D), (D // 48) ** -0.5, 1.5, ((0, 2), (1, 16))),
        "gain_feed": jnp.clip(1.0 + 0.1 * jax.random.normal(key_list[6], (D,), jnp.float32), 0.5, 1.5).astype(jnp.bfloat16),
        "w_up": noise(key_list[7], (D, FF), D ** -0.5, 0.21875, ((0, 16), (1, 2))),
        "w_down": noise(key_list[8], (FF, D), FF ** -0.5, 0.109375, ((0, 2), (1, 16))),
        "out_grad": noise(key_list[9], (SEQS, SEQ, D), 1.0, 6.0, ((0, 16), (2, 2))),
    }


@jax.custom_vjp
def low(v):
    return lax.optimization_barrier(v.astype(jnp.bfloat16)).astype(jnp.float32)

@jax.custom_vjp
def low_back(v):
    return v

def low_keep(v):
    return (low(v), None)

def low_pass(kept, grad):
    return (grad,)

def back_keep(v):
    return (v, None)

def back_low(kept, grad):
    return (low(grad),)
low.defvjp(low_keep, low_pass)
low_back.defvjp(back_keep, back_low)
EPSILON = 1e-06
MASKED = -1000000000.0
PRECISION = lax.Precision.HIGHEST

def rms_norm(values, gain):
    return values * lax.rsqrt(lax.optimization_barrier(jnp.mean(values * values, axis=-1, keepdims=True)) + EPSILON) * gain

def layer(inputs, gain_mix, w_value, mix_table, w_out, gain_feed, w_up, w_down, length):
    positions = jnp.arange(SEQ)
    live_keys = positions < length
    live_rows = live_keys.astype(jnp.float32)
    normed = low(rms_norm(inputs, gain_mix))
    value_rows = low(low_back(jnp.dot(normed, w_value, precision=PRECISION)))
    value_heads = value_rows.reshape(SEQ, HEADS, HEAD_DIM)
    scores = jnp.where(live_keys[None, None, :], mix_table, MASKED)
    probs = low(jax.nn.softmax(scores, axis=-1))
    mixed = jnp.einsum('hqk,khd->qhd', probs, value_heads, precision=PRECISION).reshape(SEQ, D)
    mixed = low(low_back(mixed))
    attended = low_back(jnp.dot(mixed, w_out, precision=PRECISION))
    hidden = inputs + attended
    normed_feed = low(rms_norm(hidden, gain_feed))
    up_proj = low_back(jnp.dot(normed_feed, w_up, precision=PRECISION))
    activated = low(jax.nn.gelu(up_proj, approximate=True))
    feed_out = jnp.dot(activated, w_down, precision=PRECISION)
    return live_rows[:, None] * (hidden + feed_out)

def reference(inputs, lengths, gain_mix, w_value, mix_table, w_out, gain_feed, w_up, w_down, out_grad):
    weights = tuple((member.astype(jnp.float32) for member in (gain_mix, w_value, mix_table, w_out, gain_feed, w_up, w_down)))

    def seq_step(totals, member):
        block_in, length, block_grad = member
        output, pullback = jax.vjp(partial(layer, length=length), block_in.astype(jnp.float32), weights[0], weights[1], weights[2], weights[3], weights[4], weights[5], weights[6])
        gradients = pullback(block_grad.astype(jnp.float32))
        totals = jax.tree.map(jnp.add, totals, tuple(gradients[1:]))
        return (totals, (output.astype(jnp.bfloat16), gradients[0].astype(jnp.bfloat16)))
    initial = tuple((jnp.zeros(member.shape, jnp.float32) for member in weights))
    totals, outputs = lax.scan(seq_step, initial, (inputs, lengths, out_grad))
    return (outputs[0], outputs[1], totals[0], totals[1], totals[2], totals[3], totals[4], totals[5], totals[6])
```

```python
from functools import partial

import jax
import jax.numpy as jnp
from jax import lax
from jax.experimental import pallas as pl
from jax.experimental.pallas import tpu as pltpu
from jax.sharding import PartitionSpec as P

EPSILON = 1e-06
GELU_C = 0.7978845608028654
GELU_K = 0.044715
PLANE = 4
HEAD_DIM = 64
VMEM = 56 * 1024 * 1024

BF16 = jnp.bfloat16
F32 = jnp.float32


def dot_nt(a, b):
    return lax.dot_general(a, b, (((1,), (1,)), ((), ())), preferred_element_type=F32)


def dot_tn(a, b):
    return lax.dot_general(a, b, (((0,), (0,)), ((), ())), preferred_element_type=F32)


def dot_nn(a, b):
    return jnp.dot(a, b, preferred_element_type=F32)


def mix_forward_kernel(core, ta, tb, v0, v1, v2, v3, masks, o0, o1, o2, o3, inv_out, e_out):
    first = core[0] == 0
    rows = ta.shape[0] * ta.shape[2]
    half = ta.shape[3]
    ea = jnp.exp(ta[:, 0].reshape(rows, half).astype(F32)).astype(BF16)
    eb = jnp.exp(tb[:, 0].reshape(rows, half).astype(F32)).astype(BF16)
    weights = jnp.concatenate([jnp.where(first, ea, eb), jnp.where(first, eb, ea)], axis=1)
    e_out[0] = weights
    seq = weights.shape[1]
    values = jnp.concatenate([v[:, 0].reshape(-1, seq) for v in (v0, v1, v2, v3)], axis=0)
    totals = dot_nt(masks[...], weights)[:8]
    inverse = 1.0 / totals
    inv_out[0] = inverse
    mixed = dot_nt(values, weights)
    for k, out in enumerate((o0, o1, o2, o3)):
        for s in range(2):
            item = 2 * k + s
            part = mixed[item * HEAD_DIM : (item + 1) * HEAD_DIM] * inverse[item : item + 1]
            out[s, 0] = part.astype(BF16)


def mix_backward_kernel(
    core, e, v0, v1, v2, v3, g0, g1, g2, g3, x0, x1, x2, x3, inv, masks,
    keep, send, w0, w1, w2, w3, total,
):
    step = pl.program_id(1)
    first = core[0] == 0
    rows = e.shape[1]
    seq = e.shape[2]
    half = seq // 2
    weights = e[0]
    scaled = []
    offsets = []
    for grad, mixed in ((g0, x0), (g1, x1), (g2, x2), (g3, x3)):
        for s in range(2):
            item = len(scaled)
            inverse = inv[0, item : item + 1]
            part = grad[s, 0].astype(F32)
            offsets.append(
                -jnp.sum(part * mixed[s, 0].astype(F32), axis=0, keepdims=True) * inverse
            )
            scaled.append((part * inverse).astype(BF16))
    offsets.append(jnp.zeros((8, rows), F32))
    scaled = jnp.concatenate(scaled, axis=0)
    offset_rows = jnp.concatenate(offsets, axis=0).astype(BF16)
    values = jnp.concatenate([v[:, 0].reshape(-1, seq) for v in (v0, v1, v2, v3)], axis=0)

    @pl.when(step == 0)
    def _():
        total[...] = jnp.zeros_like(total)

    total[...] += dot_nn(scaled, weights)
    scores = dot_tn(scaled, values) + dot_tn(offset_rows, masks[...])
    scores = weights.astype(F32) * scores
    low = scores[:, :half].astype(BF16)
    high = scores[:, half:].astype(BF16)
    shape = keep.shape[0], keep.shape[2], half
    keep[:, 0] = jnp.where(first, low, high).reshape(shape)
    send[:, 0] = jnp.where(first, high, low).reshape(shape)

    @pl.when(step == pl.num_programs(1) - 1)
    def _():
        for k, out in enumerate((w0, w1, w2, w3)):
            for s in range(2):
                item = 2 * k + s
                live = masks[item : item + 1].astype(F32)
                part = total[item * HEAD_DIM : (item + 1) * HEAD_DIM] * live
                out[s, 0] = part.astype(BF16)


def mixing_specs(blocks, block_rows, seq):
    group = max(1, 256 // block_rows)
    rows = group * block_rows
    steps = blocks // group
    half = seq // 2
    table = pl.BlockSpec((group, 1, block_rows, half), lambda h, i, c: (i, h, 0, 0))
    whole = pl.BlockSpec((2, 1, HEAD_DIM, seq), lambda h, i, c: (0, h, 0, 0))
    tokens = pl.BlockSpec((2, 1, HEAD_DIM, rows), lambda h, i, c: (0, h, 0, i))
    inverse = pl.BlockSpec((1, 8, rows), lambda h, i, c: (h, 0, i))
    expo = pl.BlockSpec((1, rows, seq), lambda h, i, c: (h, i, 0))
    masks = pl.BlockSpec((16, seq), lambda h, i, c: (0, 0))
    return steps, table, whole, tokens, inverse, expo, masks


def mix_forward(core, tab_a, tab_b, values, masks):
    blocks, heads, block_rows, half = tab_a.shape
    seq = 2 * half
    steps, table, whole, tokens, inverse, expo, mask = mixing_specs(blocks, block_rows, seq)
    piece = jax.ShapeDtypeStruct(values[0].shape, BF16)
    outs = pl.pallas_call(
        mix_forward_kernel,
        grid_spec=pltpu.PrefetchScalarGridSpec(
            num_scalar_prefetch=1,
            grid=(heads, steps),
            in_specs=[table, table] + [whole] * 4 + [mask],
            out_specs=[tokens] * 4 + [inverse, expo],
        ),
        out_shape=[piece] * 4
        + [
            jax.ShapeDtypeStruct((heads, 8, seq), F32),
            jax.ShapeDtypeStruct((heads, seq, seq), BF16),
        ],
        compiler_params=pltpu.CompilerParams(vmem_limit_bytes=VMEM),
        cost_estimate=pl.CostEstimate(
            flops=2 * heads * seq * seq * 520,
            bytes_accessed=heads * seq * seq * 4,
            transcendentals=heads * seq * seq,
        ),
    )(core, tab_a, tab_b, *values, masks)
    return outs[:4], outs[4], outs[5]


def mix_backward(core, expo_table, values, grads, mixed, inverse_sums, masks, blocks):
    heads, seq = expo_table.shape[:2]
    block_rows = seq // blocks
    half = seq // 2
    steps, table, whole, tokens, inverse, expo, mask = mixing_specs(blocks, block_rows, seq)
    piece = jax.ShapeDtypeStruct(values[0].shape, BF16)
    part = jax.ShapeDtypeStruct((blocks, heads, block_rows, half), BF16)
    outs = pl.pallas_call(
        mix_backward_kernel,
        grid_spec=pltpu.PrefetchScalarGridSpec(
            num_scalar_prefetch=1,
            grid=(heads, steps),
            in_specs=[expo] + [whole] * 4 + [tokens] * 8 + [inverse, mask],
            out_specs=[table, table] + [whole] * 4,
            scratch_shapes=[pltpu.VMEM((8 * HEAD_DIM, seq), F32)],
        ),
        out_shape=[part, part] + [piece] * 4,
        compiler_params=pltpu.CompilerParams(vmem_limit_bytes=VMEM),
        cost_estimate=pl.CostEstimate(
            flops=4 * heads * seq * seq * 520,
            bytes_accessed=heads * seq * seq * 4,
            transcendentals=0,
        ),
    )(core, expo_table, *values, *grads, *mixed, inverse_sums, masks)
    return outs[0], outs[1], outs[2:]


def feed_kernel(
    lens, hidden, grad, gain, up_a, up_b, down_a, down_b,
    out, grad_hidden, grad_low, act, grad_up, normed, gain_sum,
):
    step = pl.program_id(0)
    rows = hidden.shape[0]
    width = up_a.shape[1]
    per_item = pl.num_programs(0) // 2
    h = hidden[...]
    gains = gain[...]
    scale = lax.rsqrt(jnp.mean(h * h, axis=-1, keepdims=True) + EPSILON)
    n = (h * scale * gains).astype(BF16)
    normed[...] = n
    g = grad[...]
    feed = jnp.zeros(h.shape, F32)
    back = jnp.zeros(h.shape, F32)
    chunk = 512
    for part, (up, down) in enumerate(((up_a, down_a), (up_b, down_b))):
        for start in range(0, width, chunk):
            w_up = up[:, start : start + chunk]
            w_down = down[:, start : start + chunk]
            u = dot_nn(n, w_up)
            ga = dot_nn(g, w_down)
            square = u * u
            t = jnp.tanh(u * (GELU_C + GELU_C * GELU_K * square))
            low = 0.5 + 0.5 * t
            a = (u * low).astype(BF16)
            slope = low + (0.5 * u) * (1.0 - t * t) * (GELU_C + 3.0 * GELU_C * GELU_K * square)
            gu = (slope * ga).astype(BF16)
            where = slice(part * width + start, part * width + start + chunk)
            act[:, where] = a
            grad_up[:, where] = gu
            feed += dot_nt(a, w_down)
            back += dot_nt(gu, w_up)
    item = step // per_item
    first = (step % per_item) * rows
    position = first + lax.broadcasted_iota(jnp.int32, (rows, 1), 0)
    live = (position < lens[item]).astype(F32)
    out[...] = (live * (h + feed)).astype(BF16)
    q = back * gains
    gh = (
        g.astype(F32)
        + scale * q
        - h * (scale * scale * scale) * jnp.mean(q * h, axis=-1, keepdims=True)
    )
    grad_hidden[...] = gh
    grad_low[...] = gh.astype(BF16)
    terms = jnp.sum((back * h * scale).reshape(rows // 8, 8, -1), axis=0)

    @pl.when(step == 0)
    def _():
        gain_sum[...] = jnp.zeros_like(gain_sum)

    gain_sum[...] += terms


def feed(lens, hidden, grad, gain, up, down):
    tokens, features = hidden.shape
    width = up[0].shape[1]
    rows = 256
    steps = tokens // rows
    row = lambda n: pl.BlockSpec((rows, n), lambda i, c: (i, 0))
    fixed = lambda shape: pl.BlockSpec(shape, lambda i, c: (0, 0), pipeline_mode=pl.Buffered(1))
    shape = lambda n, d: jax.ShapeDtypeStruct((tokens, n), d)
    return pl.pallas_call(
        feed_kernel,
        grid_spec=pltpu.PrefetchScalarGridSpec(
            num_scalar_prefetch=1,
            grid=(steps,),
            in_specs=[row(features), row(features), fixed((1, features))]
            + [fixed((features, width))] * 4,
            out_specs=[
                row(features),
                row(features),
                row(features),
                row(2 * width),
                row(2 * width),
                row(features),
                pl.BlockSpec((8, features), lambda i, c: (0, 0)),
            ],
        ),
        out_shape=[
            shape(features, BF16),
            shape(features, F32),
            shape(features, BF16),
            shape(2 * width, BF16),
            shape(2 * width, BF16),
            shape(features, BF16),
            jax.ShapeDtypeStruct((8, features), F32),
        ],
        compiler_params=pltpu.CompilerParams(vmem_limit_bytes=VMEM),
        cost_estimate=pl.CostEstimate(
            flops=2 * 4 * tokens * features * 2 * width,
            bytes_accessed=tokens * (features * 16 + 8 * width) + features * width * 8,
            transcendentals=tokens * 2 * width,
        ),
    )(lens, hidden, grad, gain, *up, *down)


def body(inputs, lengths, gain_mix, w_value, mix_table, w_out, gain_feed, w_up, w_down, out_grad):
    ranks = lax.axis_size("dp")
    blocks = ranks // PLANE
    rank = lax.axis_index("dp")
    core = lax.axis_index("head")
    place = rank % PLANE
    items, seq, feature_part = inputs.shape
    mine = items // 2
    features = 2 * feature_part
    first = core == 0
    core_ref = core.astype(jnp.int32).reshape(1)
    lines = [[b * PLANE + q for b in range(blocks)] for q in range(PLANE)]

    def sibling(t):
        return lax.ppermute(t, "head", [(0, 1), (1, 0)])

    def plane(t, k):
        return lax.ppermute(t, "dp", [(i, i ^ k) for i in range(ranks)])

    def ordered(parts, axis):
        odd, far = place % 2 == 1, place >= 2
        near = [jnp.where(odd, parts[1], parts[0]), jnp.where(odd, parts[0], parts[1])]
        rest = [jnp.where(odd, parts[3], parts[2]), jnp.where(odd, parts[2], parts[3])]
        out = [jnp.where(far, b, a) for a, b in zip(near, rest)]
        out += [jnp.where(far, a, b) for a, b in zip(near, rest)]
        return jnp.stack(out, axis)

    def exchange(parts):
        return [parts[0]] + [plane(parts[k], k) for k in range(1, PLANE)]

    def pick(t, axis):
        return [
            lax.dynamic_index_in_dim(t, place ^ k, axis, keepdims=False) for k in range(PLANE)
        ]

    def both(own, other, axis):
        return jnp.where(
            first,
            jnp.concatenate([own, other], axis),
            jnp.concatenate([other, own], axis),
        )

    def halves(t, axis):
        size = t.shape[axis] // 2
        own = lax.dynamic_slice_in_dim(t, core * size, size, axis)
        return own, lax.dynamic_slice_in_dim(t, (1 - core) * size, size, axis)

    shard = gain_mix.shape[0]
    gains = jnp.pad(jnp.stack([gain_mix, gain_feed], 1), ((0, 0), (0, 126)))
    pack_first = jnp.concatenate([w_value, w_out.T, gains], 1)
    pack_first = lax.all_gather(pack_first, "dp", axis=0, tiled=True)

    table_own, table_other = halves(mix_table, 2)
    table_other = sibling(table_other)
    table = both(table_own, table_other, 0)
    heads = table.shape[0] // PLANE
    local_rows = table.shape[1]
    half = seq // 2
    table = table.reshape(PLANE, heads, local_rows, half)
    table = ordered(exchange(pick(table, 0)), 1).reshape(heads, PLANE * local_rows, half)
    table = lax.all_gather(table, "dp", axis=0, axis_index_groups=lines)

    pack_feed = jnp.concatenate([w_up, w_down.T], 1)
    pack_feed = lax.all_gather(pack_feed, "dp", axis=0, tiled=True)
    table_mate = sibling(table)

    own_in, other_in = halves(inputs, 0)
    own_grad, other_grad = halves(out_grad, 0)
    lens, _ = halves(lengths, 0)
    live = lax.iota(jnp.int32, seq)[None, :] < lens[:, None]
    x = both(own_in, sibling(other_in), 2).astype(F32)
    grad_rows = jnp.where(live[:, :, None], both(own_grad, sibling(other_grad), 2), 0)
    group_lens = jnp.stack(exchange([lens] * PLANE)).reshape(-1)
    masks = (lax.iota(jnp.int32, seq)[None, :] < group_lens[:, None]).astype(BF16)
    masks = jnp.pad(masks, ((0, 8), (0, 0)))

    value_part = w_value.shape[1]
    first_other = sibling(pack_first)
    w_value = both(pack_first[:, :value_part], first_other[:, :value_part], 1)
    w_out_t = both(
        pack_first[:, value_part : 2 * value_part],
        first_other[:, value_part : 2 * value_part],
        1,
    )
    gain_mix = pack_first[:, 2 * value_part].astype(F32)
    gain_feed = pack_first[:, 2 * value_part + 1].astype(F32)

    scale_mix = lax.rsqrt(jnp.mean(x * x, axis=-1, keepdims=True) + EPSILON)
    normed = (x * scale_mix * gain_mix).astype(BF16)
    value = jnp.einsum("sti,ic->sct", normed, w_value, preferred_element_type=F32)
    value = jnp.where(live[:, None, :], value, 0.0).astype(BF16)
    value = value.reshape(mine, PLANE, heads, HEAD_DIM, seq)
    values = exchange(pick(value, 1))

    mixed_parts, inverse_sums, expo_table = mix_forward(core_ref, table, table_mate, values, masks)
    mixed = ordered(exchange(mixed_parts), 1).reshape(mine, features, seq)
    hidden = x + jnp.einsum("sct,oc->sto", mixed, w_out_t, preferred_element_type=F32)

    feed_other = sibling(pack_feed)
    width = w_up.shape[1]
    up = (pack_feed[:, :width], feed_other[:, :width])
    down = (pack_feed[:, width:], feed_other[:, width:])
    flat = lambda t: t.reshape(-1, t.shape[-1])
    output, grad_hidden, grad_low, act, grad_up, normed_feed, feed_gain_terms = feed(
        lens, flat(hidden), flat(grad_rows), gain_feed[None], up, down
    )
    grad_low = grad_low.reshape(mine, seq, features)

    grad_mixed = jnp.einsum("sto,oc->sct", grad_low, w_out_t, preferred_element_type=F32)
    grad_mixed = grad_mixed.astype(BF16).reshape(mine, PLANE, heads, HEAD_DIM, seq)
    grads = exchange(pick(grad_mixed, 1))
    keep, send, value_parts = mix_backward(
        core_ref, expo_table, values, grads, mixed_parts, inverse_sums, masks, blocks
    )

    table_grad = (keep.astype(F32) + sibling(send).astype(F32)).astype(BF16)
    table_grad = lax.psum_scatter(
        table_grad, "dp", scatter_dimension=0, axis_index_groups=lines, tiled=False
    )
    table_grad = table_grad.reshape(heads, PLANE, local_rows, half)
    table_grad = ordered(exchange(pick(table_grad, 1)), 0)
    table_grad = table_grad.reshape(PLANE * heads, local_rows, half)
    table_own, table_other = halves(table_grad, 0)
    table_grad = both(table_own, sibling(table_other), 2).astype(F32)

    up_grad = jnp.einsum("ti,tf->if", normed_feed, grad_up, preferred_element_type=F32)
    down_grad = jnp.einsum("ti,tf->if", flat(grad_rows), act, preferred_element_type=F32)
    own = jnp.concatenate([up_grad[:, :width], down_grad[:, :width]], 1)
    other = jnp.concatenate([up_grad[:, width:], down_grad[:, width:]], 1).astype(BF16)
    own = (own + sibling(other).astype(F32)).astype(BF16)
    own = lax.psum_scatter(own, "dp", scatter_dimension=0, tiled=True).astype(F32)
    up_grad, down_grad = own[:, :width], own[:, width:].T

    grad_value = ordered(exchange(value_parts), 1).reshape(mine, features, seq)
    value_grad = jnp.einsum("sti,sct->ic", normed, grad_value, preferred_element_type=F32)
    projection_grad = jnp.einsum("sto,sct->oc", grad_low, mixed, preferred_element_type=F32)
    grad_norm = jnp.einsum("sct,ic->sti", grad_value, w_value, preferred_element_type=F32)
    mix_gain_grad = jnp.sum(grad_norm * x * scale_mix, axis=(0, 1))
    feed_gain_grad = jnp.sum(feed_gain_terms, axis=0)
    scaled = grad_norm * gain_mix
    grad_in = (
        grad_hidden.reshape(x.shape)
        + scale_mix * scaled
        - x * (scale_mix * scale_mix * scale_mix) * jnp.mean(scaled * x, axis=-1, keepdims=True)
    )

    gain_grads = jnp.pad(jnp.stack([mix_gain_grad, feed_gain_grad], 1), ((0, 0), (0, 126)))
    gain_grads = gain_grads.astype(BF16)
    value_own, value_other = halves(value_grad, 1)
    projection_own, projection_other = halves(projection_grad, 1)
    other = jnp.concatenate(
        [value_other.astype(BF16), projection_other.astype(BF16), gain_grads], 1
    )
    own = jnp.concatenate([value_own, projection_own, gain_grads.astype(F32)], 1)
    own = (own + sibling(other).astype(F32)).astype(BF16)
    own = lax.psum_scatter(own, "dp", scatter_dimension=0, tiled=True).astype(F32)
    value_grad = own[:, :value_part]
    projection_grad = own[:, value_part : 2 * value_part].T
    mix_gain_grad = own[:, 2 * value_part]
    feed_gain_grad = own[:, 2 * value_part + 1]

    def placed(t):
        kept, sent = halves(t, 2)
        return both(kept, sibling(sent), 0)

    return (
        placed(output.reshape(mine, seq, features)),
        placed(grad_in.astype(BF16)),
        mix_gain_grad,
        value_grad,
        table_grad,
        projection_grad,
        feed_gain_grad,
        up_grad,
        down_grad,
    )


def solution(mesh):
    return jax.shard_map(
        body,
        mesh=mesh,
        in_specs=(
            P("dp", None, "head"),
            P("dp"),
            P("dp"),
            P("dp", "head"),
            P("head", "dp", None),
            P("head", "dp"),
            P("dp"),
            P("dp", "head"),
            P("head", "dp"),
            P("dp", None, "head"),
        ),
        out_specs=(
            P("dp", None, "head"),
            P("dp", None, "head"),
            P("dp"),
            P("dp", "head"),
            P("head", "dp", None),
            P("head", "dp"),
            P("dp"),
            P("dp", "head"),
            P("head", "dp"),
        ),
        check_vma=False,
    )
```

```python
from functools import partial

import jax
import jax.numpy as jnp
from jax import lax
from jax.experimental import pallas as pl
from jax.experimental.pallas import tpu as pltpu
from jax.sharding import PartitionSpec as P

EPSILON = 1e-06
GELU_C = 0.7978845608028654
GELU_K = 0.044715
PLANE = 4
HEAD_DIM = 64
VMEM = 56 * 1024 * 1024

BF16 = jnp.bfloat16
F32 = jnp.float32


def dot_nt(a, b):
    return lax.dot_general(a, b, (((1,), (1,)), ((), ())), preferred_element_type=F32)


def dot_tn(a, b):
    return lax.dot_general(a, b, (((0,), (0,)), ((), ())), preferred_element_type=F32)


def dot_nn(a, b):
    return jnp.dot(a, b, preferred_element_type=F32)


def mix_forward_kernel(core, ta, tb, v0, v1, v2, v3, masks, o0, o1, o2, o3, inv_out, e_out):
    first = core[0] == 0
    rows = ta.shape[0] * ta.shape[2]
    half = ta.shape[3]
    ea = jnp.exp(ta[:, 0].reshape(rows, half).astype(F32)).astype(BF16)
    eb = jnp.exp(tb[:, 0].reshape(rows, half).astype(F32)).astype(BF16)
    weights = jnp.concatenate([jnp.where(first, ea, eb), jnp.where(first, eb, ea)], axis=1)
    e_out[0] = weights
    seq = weights.shape[1]
    values = jnp.concatenate([v[:, 0].reshape(-1, seq) for v in (v0, v1, v2, v3)], axis=0)
    totals = dot_nt(masks[...], weights)[:8]
    inverse = 1.0 / totals
    inv_out[0] = inverse
    mixed = dot_nt(values, weights)
    for k, out in enumerate((o0, o1, o2, o3)):
        for s in range(2):
            item = 2 * k + s
            part = mixed[item * HEAD_DIM : (item + 1) * HEAD_DIM] * inverse[item : item + 1]
            out[s, 0] = part.astype(BF16)


def mix_backward_kernel(
    core, e, v0, v1, v2, v3, g0, g1, g2, g3, x0, x1, x2, x3, inv, masks,
    keep, send, w0, w1, w2, w3, total,
):
    step = pl.program_id(1)
    first = core[0] == 0
    rows = e.shape[1]
    seq = e.shape[2]
    half = seq // 2
    weights = e[0]
    scaled = []
    offsets = []
    for grad, mixed in ((g0, x0), (g1, x1), (g2, x2), (g3, x3)):
        for s in range(2):
            item = len(scaled)
            inverse = inv[0, item : item + 1]
            part = grad[s, 0].astype(F32)
            offsets.append(
                -jnp.sum(part * mixed[s, 0].astype(F32), axis=0, keepdims=True) * inverse
            )
            scaled.append((part * inverse).astype(BF16))
    offsets.append(jnp.zeros((8, rows), F32))
    scaled = jnp.concatenate(scaled, axis=0)
    offset_rows = jnp.concatenate(offsets, axis=0).astype(BF16)
    values = jnp.concatenate([v[:, 0].reshape(-1, seq) for v in (v0, v1, v2, v3)], axis=0)

    @pl.when(step == 0)
    def _():
        total[...] = jnp.zeros_like(total)

    total[...] += dot_nn(scaled, weights)
    scores = dot_tn(scaled, values) + dot_tn(offset_rows, masks[...])
    scores = weights.astype(F32) * scores
    low = scores[:, :half].astype(BF16)
    high = scores[:, half:].astype(BF16)
    shape = keep.shape[0], keep.shape[2], half
    keep[:, 0] = jnp.where(first, low, high).reshape(shape)
    send[:, 0] = jnp.where(first, high, low).reshape(shape)

    @pl.when(step == pl.num_programs(1) - 1)
    def _():
        for k, out in enumerate((w0, w1, w2, w3)):
            for s in range(2):
                item = 2 * k + s
                live = masks[item : item + 1].astype(F32)
                part = total[item * HEAD_DIM : (item + 1) * HEAD_DIM] * live
                out[s, 0] = part.astype(BF16)


def mixing_specs(blocks, block_rows, seq):
    group = max(1, 256 // block_rows)
    rows = group * block_rows
    steps = blocks // group
    half = seq // 2
    table = pl.BlockSpec((group, 1, block_rows, half), lambda h, i, c: (i, h, 0, 0))
    whole = pl.BlockSpec((2, 1, HEAD_DIM, seq), lambda h, i, c: (0, h, 0, 0))
    tokens = pl.BlockSpec((2, 1, HEAD_DIM, rows), lambda h, i, c: (0, h, 0, i))
    inverse = pl.BlockSpec((1, 8, rows), lambda h, i, c: (h, 0, i))
    expo = pl.BlockSpec((1, rows, seq), lambda h, i, c: (h, i, 0))
    masks = pl.BlockSpec((16, seq), lambda h, i, c: (0, 0))
    return steps, table, whole, tokens, inverse, expo, masks


def mix_forward(core, tab_a, tab_b, values, masks):
    blocks, heads, block_rows, half = tab_a.shape
    seq = 2 * half
    steps, table, whole, tokens, inverse, expo, mask = mixing_specs(blocks, block_rows, seq)
    piece = jax.ShapeDtypeStruct(values[0].shape, BF16)
    outs = pl.pallas_call(
        mix_forward_kernel,
        grid_spec=pltpu.PrefetchScalarGridSpec(
            num_scalar_prefetch=1,
            grid=(heads, steps),
            in_specs=[table, table] + [whole] * 4 + [mask],
            out_specs=[tokens] * 4 + [inverse, expo],
        ),
        out_shape=[piece] * 4
        + [
            jax.ShapeDtypeStruct((heads, 8, seq), F32),
            jax.ShapeDtypeStruct((heads, seq, seq), BF16),
        ],
        compiler_params=pltpu.CompilerParams(vmem_limit_bytes=VMEM),
        cost_estimate=pl.CostEstimate(
            flops=2 * heads * seq * seq * 520,
            bytes_accessed=heads * seq * seq * 4,
            transcendentals=heads * seq * seq,
        ),
    )(core, tab_a, tab_b, *values, masks)
    return outs[:4], outs[4], outs[5]


def mix_backward(core, expo_table, values, grads, mixed, inverse_sums, masks, blocks):
    heads, seq = expo_table.shape[:2]
    block_rows = seq // blocks
    half = seq // 2
    steps, table, whole, tokens, inverse, expo, mask = mixing_specs(blocks, block_rows, seq)
    piece = jax.ShapeDtypeStruct(values[0].shape, BF16)
    part = jax.ShapeDtypeStruct((blocks, heads, block_rows, half), BF16)
    outs = pl.pallas_call(
        mix_backward_kernel,
        grid_spec=pltpu.PrefetchScalarGridSpec(
            num_scalar_prefetch=1,
            grid=(heads, steps),
            in_specs=[expo] + [whole] * 4 + [tokens] * 8 + [inverse, mask],
            out_specs=[table, table] + [whole] * 4,
            scratch_shapes=[pltpu.VMEM((8 * HEAD_DIM, seq), F32)],
        ),
        out_shape=[part, part] + [piece] * 4,
        compiler_params=pltpu.CompilerParams(vmem_limit_bytes=VMEM),
        cost_estimate=pl.CostEstimate(
            flops=4 * heads * seq * seq * 520,
            bytes_accessed=heads * seq * seq * 4,
            transcendentals=0,
        ),
    )(core, expo_table, *values, *grads, *mixed, inverse_sums, masks)
    return outs[0], outs[1], outs[2:]


def feed_kernel(
    lens, hidden, grad, gain, up_a, up_b, down_a, down_b,
    out, grad_hidden, grad_low, act, grad_up, normed, gain_sum,
):
    step = pl.program_id(0)
    rows = hidden.shape[0]
    width = up_a.shape[1]
    per_item = pl.num_programs(0) // 2
    h = hidden[...]
    gains = gain[...]
    scale = lax.rsqrt(jnp.mean(h * h, axis=-1, keepdims=True) + EPSILON)
    n = (h * scale * gains).astype(BF16)
    normed[...] = n
    g = grad[...]
    feed = jnp.zeros(h.shape, F32)
    back = jnp.zeros(h.shape, F32)
    chunk = 512
    for part, (up, down) in enumerate(((up_a, down_a), (up_b, down_b))):
        for start in range(0, width, chunk):
            w_up = up[:, start : start + chunk]
            w_down = down[:, start : start + chunk]
            u = dot_nn(n, w_up)
            ga = dot_nn(g, w_down)
            square = u * u
            t = jnp.tanh(u * (GELU_C + GELU_C * GELU_K * square))
            low = 0.5 + 0.5 * t
            a = (u * low).astype(BF16)
            slope = low + (0.5 * u) * (1.0 - t * t) * (GELU_C + 3.0 * GELU_C * GELU_K * square)
            gu = (slope * ga).astype(BF16)
            where = slice(part * width + start, part * width + start + chunk)
            act[:, where] = a
            grad_up[:, where] = gu
            feed += dot_nt(a, w_down)
            back += dot_nt(gu, w_up)
    item = step // per_item
    first = (step % per_item) * rows
    position = first + lax.broadcasted_iota(jnp.int32, (rows, 1), 0)
    live = (position < lens[item]).astype(F32)
    out[...] = (live * (h + feed)).astype(BF16)
    q = back * gains
    gh = (
        g.astype(F32)
        + scale * q
        - h * (scale * scale * scale) * jnp.mean(q * h, axis=-1, keepdims=True)
    )
    grad_hidden[...] = gh
    grad_low[...] = gh.astype(BF16)
    terms = jnp.sum((back * h * scale).reshape(rows // 8, 8, -1), axis=0)

    @pl.when(step == 0)
    def _():
        gain_sum[...] = jnp.zeros_like(gain_sum)

    gain_sum[...] += terms


def feed(lens, hidden, grad, gain, up, down):
    tokens, features = hidden.shape
    width = up[0].shape[1]
    rows = 256
    steps = tokens // rows
    row = lambda n: pl.BlockSpec((rows, n), lambda i, c: (i, 0))
    fixed = lambda shape: pl.BlockSpec(shape, lambda i, c: (0, 0), pipeline_mode=pl.Buffered(1))
    shape = lambda n, d: jax.ShapeDtypeStruct((tokens, n), d)
    return pl.pallas_call(
        feed_kernel,
        grid_spec=pltpu.PrefetchScalarGridSpec(
            num_scalar_prefetch=1,
            grid=(steps,),
            in_specs=[row(features), row(features), fixed((1, features))]
            + [fixed((features, width))] * 4,
            out_specs=[
                row(features),
                row(features),
                row(features),
                row(2 * width),
                row(2 * width),
                row(features),
                pl.BlockSpec((8, features), lambda i, c: (0, 0)),
            ],
        ),
        out_shape=[
            shape(features, BF16),
            shape(features, F32),
            shape(features, BF16),
            shape(2 * width, BF16),
            shape(2 * width, BF16),
            shape(features, BF16),
            jax.ShapeDtypeStruct((8, features), F32),
        ],
        compiler_params=pltpu.CompilerParams(vmem_limit_bytes=VMEM),
        cost_estimate=pl.CostEstimate(
            flops=2 * 4 * tokens * features * 2 * width,
            bytes_accessed=tokens * (features * 16 + 8 * width) + features * width * 8,
            transcendentals=tokens * 2 * width,
        ),
    )(lens, hidden, grad, gain, *up, *down)


def body(inputs, lengths, gain_mix, w_value, mix_table, w_out, gain_feed, w_up, w_down, out_grad):
    ranks = lax.axis_size("dp")
    blocks = ranks // PLANE
    rank = lax.axis_index("dp")
    core = lax.axis_index("head")
    place = rank % PLANE
    items, seq, feature_part = inputs.shape
    mine = items // 2
    features = 2 * feature_part
    first = core == 0
    core_ref = core.astype(jnp.int32).reshape(1)
    cube_bits = [1 << b for b in range(ranks.bit_length() - 2, -1, -1)]
    lines = [[b * PLANE + q for b in range(blocks)] for q in range(PLANE)]

    def sibling(t):
        return lax.ppermute(t, "head", [(0, 1), (1, 0)])

    def chip(t, k):
        return lax.ppermute(t, "dp", [(i, i ^ k) for i in range(ranks)])

    def ordered(parts, axis):
        odd, far = place % 2 == 1, place >= 2
        near = [jnp.where(odd, parts[1], parts[0]), jnp.where(odd, parts[0], parts[1])]
        rest = [jnp.where(odd, parts[3], parts[2]), jnp.where(odd, parts[2], parts[3])]
        out = [jnp.where(far, b, a) for a, b in zip(near, rest)]
        out += [jnp.where(far, a, b) for a, b in zip(near, rest)]
        return jnp.stack(out, axis)

    def exchange(parts):
        return [parts[0]] + [chip(parts[k], k) for k in range(1, PLANE)]

    def pick(t, axis):
        return [
            lax.dynamic_index_in_dim(t, place ^ k, axis, keepdims=False) for k in range(PLANE)
        ]

    def both(own, other, axis):
        return jnp.where(
            first,
            jnp.concatenate([own, other], axis),
            jnp.concatenate([other, own], axis),
        )

    def halves(t, axis):
        size = t.shape[axis] // 2
        own = lax.dynamic_slice_in_dim(t, core * size, size, axis)
        return own, lax.dynamic_slice_in_dim(t, (1 - core) * size, size, axis)

    def cube_gather(t):
        rows = t.shape[0]
        axis = 0
        for bit in cube_bits:
            got = chip(t, bit)
            upper = (rank & bit) != 0
            t = jnp.where(upper, jnp.stack([got, t], axis), jnp.stack([t, got], axis))
            axis += 1
        return t.reshape(ranks * rows, -1)

    def cube_fold(t, axis, bit):
        upper = ((rank & bit) != 0).astype(jnp.int32)
        sent = lax.dynamic_index_in_dim(t, 1 - upper, axis, keepdims=False)
        kept = lax.dynamic_index_in_dim(t, upper, axis, keepdims=False)
        return kept.astype(F32) + chip(sent.astype(BF16), bit).astype(F32)

    def cube_scatter(t):
        t = t.reshape((2,) * len(cube_bits) + (t.shape[0] // ranks, t.shape[1]))
        for axis in range(len(cube_bits) - 1, -1, -1):
            t = cube_fold(t, axis, cube_bits[axis])
        return t

    gains = jnp.pad(jnp.stack([gain_mix, gain_feed], 1), ((0, 0), (0, 126)))
    pack_first = jnp.concatenate([w_value, w_out.T, gains], 1)
    pack_first = cube_gather(pack_first)

    table_own, table_other = halves(mix_table, 2)
    table_other = sibling(table_other)
    table = both(table_own, table_other, 0)
    heads = table.shape[0] // PLANE
    local_rows = table.shape[1]
    half = seq // 2
    table = table.reshape(PLANE, heads, local_rows, half)
    table = ordered(exchange(pick(table, 0)), 1).reshape(heads, PLANE * local_rows, half)
    table = lax.all_gather(table, "dp", axis=0, axis_index_groups=lines)

    pack_feed = jnp.concatenate([w_up, w_down.T], 1)
    pack_feed, table = lax.optimization_barrier((pack_feed, table))
    pack_feed = lax.all_gather(pack_feed, "dp", axis=0, tiled=True)
    table_mate = sibling(table)

    own_in, other_in = halves(inputs, 0)
    own_grad, other_grad = halves(out_grad, 0)
    lens, _ = halves(lengths, 0)
    live = lax.iota(jnp.int32, seq)[None, :] < lens[:, None]
    x = both(own_in, sibling(other_in), 2).astype(F32)
    grad_rows = jnp.where(live[:, :, None], both(own_grad, sibling(other_grad), 2), 0)
    group_lens = jnp.stack(exchange([lens] * PLANE)).reshape(-1)
    masks = (lax.iota(jnp.int32, seq)[None, :] < group_lens[:, None]).astype(BF16)
    masks = jnp.pad(masks, ((0, 8), (0, 0)))

    value_part = w_value.shape[1]
    first_other = sibling(pack_first)
    w_value = both(pack_first[:, :value_part], first_other[:, :value_part], 1)
    w_out_t = both(
        pack_first[:, value_part : 2 * value_part],
        first_other[:, value_part : 2 * value_part],
        1,
    )
    gain_mix = pack_first[:, 2 * value_part].astype(F32)
    gain_feed = pack_first[:, 2 * value_part + 1].astype(F32)

    scale_mix = lax.rsqrt(jnp.mean(x * x, axis=-1, keepdims=True) + EPSILON)
    normed = (x * scale_mix * gain_mix).astype(BF16)
    value = jnp.einsum("sti,ic->sct", normed, w_value, preferred_element_type=F32)
    value = jnp.where(live[:, None, :], value, 0.0).astype(BF16)
    value = value.reshape(mine, PLANE, heads, HEAD_DIM, seq)
    values = exchange(pick(value, 1))

    mixed_parts, inverse_sums, expo_table = mix_forward(core_ref, table, table_mate, values, masks)
    mixed = ordered(exchange(mixed_parts), 1).reshape(mine, features, seq)
    hidden = x + jnp.einsum("sct,oc->sto", mixed, w_out_t, preferred_element_type=F32)

    feed_other = sibling(pack_feed)
    width = w_up.shape[1]
    up = (pack_feed[:, :width], feed_other[:, :width])
    down = (pack_feed[:, width:], feed_other[:, width:])
    flat = lambda t: t.reshape(-1, t.shape[-1])
    output, grad_hidden, grad_low, act, grad_up, normed_feed, feed_gain_terms = feed(
        lens, flat(hidden), flat(grad_rows), gain_feed[None], up, down
    )
    grad_low = grad_low.reshape(mine, seq, features)

    grad_mixed = jnp.einsum("sto,oc->sct", grad_low, w_out_t, preferred_element_type=F32)
    grad_mixed = grad_mixed.astype(BF16).reshape(mine, PLANE, heads, HEAD_DIM, seq)
    grads = exchange(pick(grad_mixed, 1))
    keep, send, value_parts = mix_backward(
        core_ref, expo_table, values, grads, mixed_parts, inverse_sums, masks, blocks
    )

    table_grad = (keep.astype(F32) + sibling(send).astype(F32)).astype(BF16)
    table_grad = lax.psum_scatter(
        table_grad, "dp", scatter_dimension=0, axis_index_groups=lines, tiled=False
    )
    table_grad = table_grad.reshape(heads, PLANE, local_rows, half)
    table_grad = ordered(exchange(pick(table_grad, 1)), 0)
    table_grad = table_grad.reshape(PLANE * heads, local_rows, half)
    table_own, table_other = halves(table_grad, 0)
    table_grad = both(table_own, sibling(table_other), 2).astype(F32)

    up_grad = jnp.einsum("ti,tf->if", normed_feed, grad_up, preferred_element_type=F32)
    down_grad = jnp.einsum("ti,tf->if", flat(grad_rows), act, preferred_element_type=F32)
    parts = []
    for grad, order in ((up_grad, ((2, 1), (1, 2))), (down_grad, ((1, 2), (1, 1)))):
        part = grad[:, :width] + sibling(grad[:, width:].astype(BF16)).astype(F32)
        part = part.reshape(blocks, 2, 2, -1, width)
        for axis, bit in order:
            part = cube_fold(part, axis, bit)
        parts.append(part.astype(BF16))
    parts = lax.psum_scatter(
        jnp.concatenate(parts, 2), "dp", scatter_dimension=0, axis_index_groups=lines, tiled=False
    ).astype(F32)
    up_grad, down_grad = parts[:, :width], parts[:, width:].T

    grad_value = ordered(exchange(value_parts), 1).reshape(mine, features, seq)
    value_grad = jnp.einsum("sti,sct->ic", normed, grad_value, preferred_element_type=F32)
    projection_grad = jnp.einsum("sto,sct->oc", grad_low, mixed, preferred_element_type=F32)
    grad_norm = jnp.einsum("sct,ic->sti", grad_value, w_value, preferred_element_type=F32)
    mix_gain_grad = jnp.sum(grad_norm * x * scale_mix, axis=(0, 1))
    feed_gain_grad = jnp.sum(feed_gain_terms, axis=0)
    scaled = grad_norm * gain_mix
    grad_in = (
        grad_hidden.reshape(x.shape)
        + scale_mix * scaled
        - x * (scale_mix * scale_mix * scale_mix) * jnp.mean(scaled * x, axis=-1, keepdims=True)
    )

    gain_grads = jnp.pad(jnp.stack([mix_gain_grad, feed_gain_grad], 1), ((0, 0), (0, 126)))
    gain_grads = gain_grads.astype(BF16)
    value_own, value_other = halves(value_grad, 1)
    projection_own, projection_other = halves(projection_grad, 1)
    other = jnp.concatenate(
        [value_other.astype(BF16), projection_other.astype(BF16), gain_grads], 1
    )
    own = jnp.concatenate([value_own, projection_own, gain_grads.astype(F32)], 1)
    own = cube_scatter(own + sibling(other).astype(F32))
    value_grad = own[:, :value_part]
    projection_grad = own[:, value_part : 2 * value_part].T
    mix_gain_grad = own[:, 2 * value_part]
    feed_gain_grad = own[:, 2 * value_part + 1]

    def placed(t):
        kept, sent = halves(t, 2)
        return both(kept, sibling(sent), 0)

    return (
        placed(output.reshape(mine, seq, features)),
        placed(grad_in.astype(BF16)),
        mix_gain_grad,
        value_grad,
        table_grad,
        projection_grad,
        feed_gain_grad,
        up_grad,
        down_grad,
    )


def solution(mesh):
    return jax.shard_map(
        body,
        mesh=mesh,
        in_specs=(
            P("dp", None, "head"),
            P("dp"),
            P("dp"),
            P("dp", "head"),
            P("head", "dp", None),
            P("head", "dp"),
            P("dp"),
            P("dp", "head"),
            P("head", "dp"),
            P("dp", None, "head"),
        ),
        out_specs=(
            P("dp", None, "head"),
            P("dp", None, "head"),
            P("dp"),
            P("dp", "head"),
            P("head", "dp", None),
            P("head", "dp"),
            P("dp"),
            P("dp", "head"),
            P("head", "dp"),
        ),
        check_vma=False,
    )
```
